512 devices in a mesh: ctx: 32 (over y, z_lo), head: 16 (over z_hi, x, core).
Axes of the slice: x: 4, y: 4, z: 16 (z_hi: 2, z_lo: 8; z = z_hi * 8 + z_lo), core: 2. Of those that a mesh axis runs over, the one named last changes fastest.
Arguments:
- query_rows: bfloat16 [12288, 16, 128], P('ctx', 'head'), may hold values from -5 to 5
- key_rows: bfloat16 [12288, 16, 128], P('ctx', 'head'), may hold values from -5 to 5
- value_rows: bfloat16 [12288, 16, 128], P('ctx', 'head'), may hold values from -6 to 6
- out_weight: bfloat16 [2048, 2048], P('head'), may hold values from -0.1875 to 0.1875
Outputs:
- projected: bfloat16 [12288, 2048], P('ctx', 'head')
The draws below stay inside these ranges and needn't reach their ends.
All inputs are finite; a program needn't handle non-finite values.
Results may differ from the reference program's by a relative error of at most 0.0058.
Values may be sent and summed in bfloat16 or wider, within the bound.
No kernel may reach another device: no remote copies, remote signals or barrier semaphores. Data moves between devices by JAX's collectives and lax.ppermute only.
A program may use at most 64 MiB of HBM per device.

```python
import jax
import jax.numpy as jnp
from jax import lax

HDIM = 128
HEADS = 16
MODEL = 2048
TOKENS = 12288


def draw_query_rows(key, part):
    key = jax.random.fold_in(key, 11)
    base = jnp.clip(1.6 * jax.random.normal(key, (TOKENS, HEADS, HDIM), jnp.float32), -5.0, 5.0)
    return base.astype(jnp.bfloat16)


def draw_key_rows(key, part):
    key = jax.random.fold_in(key, 23)
    base = jnp.clip(1.6 * jax.random.normal(key, (TOKENS, HEADS, HDIM), jnp.float32), -5.0, 5.0)
    return base.astype(jnp.bfloat16)


def spiked(entries, key, source, target, blocks, factor):
    def block_of(dim):
        return (jnp.arange(entries.shape[dim]) // (entries.shape[dim] // blocks)).reshape((-1,) + (1,) * (entries.ndim - 1 - dim))

    one_side = jax.random.permutation(key, blocks)[block_of(target)]
    second = (block_of(target) + blocks // 2) % blocks
    return jnp.where((block_of(source) == one_side) | (block_of(source) == second), factor * entries, entries)


def block_scale(stream_key, extent, shards, smallest, high):
    def one(axis_at, shards_of):
        steps = jax.random.uniform(jax.random.fold_in(jax.random.fold_in(stream_key, 6), axis_at), (shards_of,), jnp.float32, smallest / len(shards), high / len(shards))
        return jnp.repeat(jnp.exp(steps), extent[axis_at] // shards_of).reshape((-1,) + (1,) * (len(extent) - axis_at - 1))

    loudness = one(*shards[0])
    for cut in shards[1:]:
        loudness = loudness * one(*cut)
    return loudness


def gaussian(stream_key, extent, width, reach, shards=(), dtype=jnp.bfloat16):
    values = jax.random.normal(stream_key, extent, jnp.float32) * width
    if len(shards) > 0:
        values = block_scale(stream_key, extent, shards, -0.22, 0.18) * values
    return jnp.clip(values, min=-reach, max=reach).astype(dtype)


def noise_with(key, dims, scale, bound, cuts, heavy, kind=jnp.bfloat16):
    values = scale * jax.random.normal(key, dims, jnp.float32)
    if cuts:
        values = values * block_scale(key, dims, cuts, -0.22, 0.18)
    return jnp.clip(spiked(values, jax.random.fold_in(key, 3), *heavy), -bound, bound).astype(kind)


def setup_inputs(seed: int = 0) -> dict:
    seeds = jax.random.split(jax.random.key(seed), 5)
    query_rows = draw_query_rows(jax.random.fold_in(seeds[4], 71), 0)
    key_rows = draw_key_rows(jax.random.fold_in(seeds[4], 71), 0)
    value_rows = gaussian(seeds[2], (TOKENS, HEADS, HDIM), 1.0, 6.0, ((0, 32), (1, 16)))
    out_weight = noise_with(seeds[3], (MODEL, MODEL), MODEL ** -0.5, 0.1875, ((0, 16),), (0, 1, 16, 2.0))
    return {"query_rows": query_rows, "key_rows": key_rows, "value_rows": value_rows, "out_weight": out_weight}


def one_head(inputs):
    query_head, key_head, value_head = inputs
    scores = jnp.dot(query_head, key_head.T, preferred_element_type=jnp.float32) * (HDIM ** -0.5)
    row_peak = jnp.max(scores, axis=1)
    expo = jnp.exp(scores - row_peak[:, None])
    row_total = jnp.sum(expo, axis=1)
    shares = expo / row_total[:, None]
    column_sum = jnp.sum(shares, axis=0)
    weights = (shares / column_sum[None, :]).astype(jnp.bfloat16)
    return jnp.dot(weights, value_head, preferred_element_type=jnp.float32).astype(jnp.bfloat16)


def reference(query_rows, key_rows, value_rows, out_weight):
    by_head = (jnp.transpose(query_rows, (1, 0, 2)), jnp.transpose(key_rows, (1, 0, 2)), jnp.transpose(value_rows, (1, 0, 2)))
    attended = lax.map(one_head, by_head)
    flat = jnp.transpose(attended, (1, 0, 2)).reshape(TOKENS, MODEL)
    return jnp.dot(flat, out_weight, preferred_element_type=jnp.float32).astype(jnp.bfloat16)
```

```python
import functools
import math

import jax
import jax.numpy as jnp
from jax import lax
from jax.experimental import pallas as pl
from jax.experimental.pallas import tpu as pltpu
from jax.sharding import PartitionSpec as P

F32 = jnp.float32
BF16 = jnp.bfloat16
ROWS = 384
DIM = 128
QB = 4
KB = 8
HALF = 4 * ROWS
KEY_BITS = ((0, 2, 4, 6), (1, 3, 5, 7))
QUERY_BITS = (0, 2, 1, 3)
GROUPS = ROWS // 128
SUB = 128
EXP_SCALE = DIM ** -0.5 * math.log2(math.e)
LIFT = 2.0 ** 20
NT = (((1,), (1,)), ((), ()))
VMEM = pl.BlockSpec(memory_space=pltpu.VMEM)


def ctx_send(value, dy=0, dza=0, dzb=0):
    step = dy * 8 + dza * 4 + dzb
    return lax.ppermute(value, "ctx", [(i, i ^ step) for i in range(32)])


def head_send(value, dzh=0, dx=0, dcore=0):
    step = dzh * 8 + dx * 2 + dcore
    return lax.ppermute(value, "head", [(i, i ^ step) for i in range(16)])


LINE = [[y * 8 + za * 4 + zb for zb in range(4)] for y in range(4) for za in range(2)]
PLANE = [[y * 8 + za * 4 + zb for y in range(4) for za in range(2)] for zb in range(4)]
ROW = [[zh * 8 + x * 2 + core for x in range(4)] for zh in range(2) for core in range(2)]


def swap(value, axis, groups):
    return lax.all_to_all(value, axis, 0, 0, axis_index_groups=groups, tiled=True)


def columns_to_rows(columns):
    lane = lax.broadcasted_iota(jnp.int32, (128, 128), 1)
    square = jnp.zeros((128, 128), F32)
    for at, column in enumerate(columns):
        square = jnp.where(lane == at, column, square)
    return square.T[:8]


def rows_to_columns(rows):
    return jnp.concatenate([rows] * 16, axis=0).T


def gather_queries(u, q_refs, q_all):
    @pl.when(u == 0)
    def _():
        q_all[0] = q_refs[0][0]
        q_all[1] = q_refs[1][0]
        q_all[2] = q_refs[2][0]
        q_all[3] = q_refs[2][1]


def half_scores(u, q_all, kv_refs, e_ref, s_ref):
    peaks, totals = [], []
    for sub in range(GROUPS):
        q = q_all[u, sub * SUB : (sub + 1) * SUB, :]
        top = jnp.full((SUB, 128), -jnp.inf, F32)
        for b in range(4):
            s = lax.dot_general(q, kv_refs[b][0], NT, preferred_element_type=F32)
            s_ref[sub, :, b * ROWS : (b + 1) * ROWS] = s
            for g in range(GROUPS):
                top = jnp.maximum(top, s[:, g * 128 : (g + 1) * 128])
        peak = jnp.max(top, axis=1, keepdims=True)
        total = jnp.zeros((SUB, 128), F32)
        for b in range(4 * GROUPS):
            e = jnp.exp2((s_ref[sub, :, b * 128 : (b + 1) * 128] - peak) * EXP_SCALE)
            total = total + e
            e_ref[sub * SUB : (sub + 1) * SUB, b * 128 : (b + 1) * 128] = e.astype(BF16)
        peaks.append(peak)
        totals.append(jnp.sum(total, axis=1, keepdims=True))
    return columns_to_rows(peaks + totals)


def first_score_kernel(*refs):
    q_refs, kv_refs, (e_ref, stat_ref, q_all, s_ref) = refs[:3], refs[3:7], refs[7:]
    u = pl.program_id(0)
    gather_queries(u, q_refs, q_all)
    stat_ref[u] = half_scores(u, q_all, kv_refs, e_ref, s_ref)


def combine(a, b):
    peak = jnp.maximum(a[:GROUPS], b[:GROUPS])
    total = a[GROUPS : 2 * GROUPS] * jnp.exp2((a[:GROUPS] - peak) * EXP_SCALE)
    total = total + b[GROUPS : 2 * GROUPS] * jnp.exp2((b[:GROUPS] - peak) * EXP_SCALE)
    return jnp.concatenate([peak, total, jnp.zeros((8 - 2 * GROUPS, 128), F32)], axis=0)


def second_score_kernel(place_ref, *refs):
    q_refs, kv_refs, first_ref = refs[:3], refs[3:7], refs[7]
    e_ref, stat_ref, both_ref, q_all, s_ref = refs[8:]
    u = pl.program_id(0)
    gather_queries(u, q_refs, q_all)
    rows = half_scores(u, q_all, kv_refs, e_ref, s_ref)
    stat_ref[u] = rows
    rows = combine(first_ref[u], rows)
    at = place_ref[0] ^ ((u % 2) * 2 + u // 2)
    for to in range(QB):
        both_ref[to, at] = rows


SMEM = pl.BlockSpec(memory_space=pltpu.SMEM)
EXPO = pl.BlockSpec((ROWS, HALF), lambda u: (u, 0))
SCORE = dict(
    grid=(QB,),
    scratch_shapes=[pltpu.VMEM((QB, ROWS, DIM), BF16), pltpu.VMEM((GROUPS, SUB, HALF), F32)],
    compiler_params=pltpu.CompilerParams(vmem_limit_bytes=16 * 1024 * 1024),
)
EXPO_TYPE = jax.ShapeDtypeStruct((QB * ROWS, HALF), BF16)
STAT_TYPE = jax.ShapeDtypeStruct((QB, 8, 128), F32)


def first_scores(queries, pieces):
    return pl.pallas_call(
        first_score_kernel,
        in_specs=[VMEM] * 7,
        out_specs=[EXPO, VMEM],
        out_shape=[EXPO_TYPE, STAT_TYPE],
        **SCORE,
    )(*queries, *pieces)


def second_scores(place, queries, pieces, stats):
    return pl.pallas_call(
        second_score_kernel,
        in_specs=[SMEM] + [VMEM] * 8,
        out_specs=[EXPO, VMEM, VMEM],
        out_shape=[EXPO_TYPE, STAT_TYPE, jax.ShapeDtypeStruct((QB, QB, 8, 128), F32)],
        **SCORE,
    )(place, *queries, *pieces, stats)


def column_kernel(
    place_ref, e0_ref, e1_ref, stat0_ref, stat1_ref, all_ref, factor_ref, column_ref, sum_ref
):
    u = pl.program_id(0)

    @pl.when(u == 0)
    def _():
        for block in range(QB):
            at = place_ref[0] ^ QUERY_BITS[block]
            whole = functools.reduce(combine, [all_ref[j, at] for j in range(QB)])
            for half, stat_ref in enumerate((stat0_ref, stat1_ref)):
                mine = stat_ref[block]
                factor = jnp.exp2((mine[:GROUPS] - whole[:GROUPS]) * EXP_SCALE)
                factor = factor / whole[GROUPS : 2 * GROUPS]
                factor_ref[half, block] = jnp.concatenate(
                    [factor, jnp.zeros((8 - GROUPS, 128), F32)], axis=0
                )
        sum_ref[...] = jnp.zeros_like(sum_ref)

    at = lax.broadcasted_iota(jnp.int32, (16, ROWS), 0)
    for half, e_ref in enumerate((e0_ref, e1_ref)):
        mine = factor_ref[half, u]
        row = jnp.concatenate([mine[g : g + 1] for g in range(GROUPS)], axis=1)
        high = row.astype(BF16).astype(F32)
        left = jnp.where(at == 0, high, jnp.where(at == 1, row - high, 0.0)).astype(BF16)
        sum_ref[half] += jnp.dot(left, e_ref[...], preferred_element_type=F32)

    @pl.when(u == QB - 1)
    def _():
        for half in range(2):
            whole = sum_ref[half, 0:1] + sum_ref[half, 1:2]
            for b in range(4):
                row = whole[:, b * ROWS : (b + 1) * ROWS]
                column_ref[0, pl.ds(place_ref[1] ^ KEY_BITS[half][b], 1)] = row
        for to in range(1, KB):
            column_ref[to] = column_ref[0]


def columns(place, expos, stats, all_stats):
    return pl.pallas_call(
        column_kernel,
        grid=(QB,),
        in_specs=[SMEM, EXPO, EXPO, VMEM, VMEM, VMEM],
        out_specs=[VMEM, VMEM],
        out_shape=[
            jax.ShapeDtypeStruct((2, QB, 8, 128), F32),
            jax.ShapeDtypeStruct((KB, KB, ROWS), F32),
        ],
        scratch_shapes=[pltpu.VMEM((2, 16, HALF), F32)],
        compiler_params=pltpu.CompilerParams(vmem_limit_bytes=16 * 1024 * 1024),
    )(place, *expos, *stats, all_stats)


def value_kernel(place_ref, e0_ref, e1_ref, factor_ref, *refs):
    kv_refs, (sums_ref, out_ref, scaled, inverse) = refs[:KB], refs[KB:]
    u = pl.program_id(0)

    @pl.when(u == 0)
    def _():
        inverse[...] = (1.0 / LIFT) / functools.reduce(
            jnp.add, [sums_ref[j] for j in range(KB)]
        )
        bits = KEY_BITS[0] + KEY_BITS[1]
        rows = jnp.concatenate(
            [inverse[pl.ds(place_ref[1] ^ bit, 1)] for bit in bits], axis=0
        )
        for g in range(GROUPS):
            column = rows_to_columns(rows[:, g * 128 : (g + 1) * 128])
            for b in range(KB):
                part = kv_refs[b][1, g * 128 : (g + 1) * 128, :].astype(F32)
                scaled[b * ROWS + g * 128 : b * ROWS + (g + 1) * 128, :] = (
                    part * column[:, b : b + 1]
                ).astype(BF16)

    parts = []
    for half, e_ref in enumerate((e0_ref, e1_ref)):
        part = jnp.dot(
            e_ref[...], scaled[half * HALF : (half + 1) * HALF], preferred_element_type=F32
        )
        parts.append((part, rows_to_columns(factor_ref[half, u]) * LIFT))
    at = place_ref[0] ^ ((u % 2) * 2 + u // 2)
    for g in range(GROUPS):
        rows = slice(g * 128, (g + 1) * 128)
        out_ref[at, rows, :] = sum(
            part[rows] * column[:, g : g + 1] for part, column in parts
        ).astype(BF16)


def attend(place, expos, factor, pieces, sums):
    return pl.pallas_call(
        value_kernel,
        grid=(QB,),
        in_specs=[SMEM, EXPO, EXPO] + [VMEM] * (KB + 2),
        out_specs=VMEM,
        out_shape=jax.ShapeDtypeStruct((QB, ROWS, DIM), BF16),
        scratch_shapes=[pltpu.VMEM((2 * HALF, DIM), BF16), pltpu.VMEM((KB, ROWS), F32)],
        compiler_params=pltpu.CompilerParams(vmem_limit_bytes=16 * 1024 * 1024),
    )(place, *expos, factor, *pieces, sums)


def weight_kernel(place_ref, w_ref, *outs):
    zh, x, core = place_ref[2], place_ref[3], place_ref[4]
    for dx in range(4):
        for dcore in range(2):
            for dzh in range(2):
                to = (zh ^ dzh) * 8 + (x ^ dx) * 2 + (core ^ dcore)
                at = dcore * 2 + dzh
                outs[dx][:, at * 128 : (at + 1) * 128] = w_ref[
                    :, pl.ds(pl.multiple_of(to * 128, 128), 128)
                ]


def weight_parts(place, out_weight):
    return pl.pallas_call(
        weight_kernel,
        in_specs=[SMEM, VMEM],
        out_specs=[VMEM] * 4,
        out_shape=[jax.ShapeDtypeStruct((DIM, 512), BF16)] * 4,
        compiler_params=pltpu.CompilerParams(vmem_limit_bytes=8 * 1024 * 1024),
    )(place, out_weight)


def project_kernel(place_ref, rows_ref, *refs):
    weights, (keep_ref, send_ref) = refs[:4], refs[4:]
    total = jnp.zeros((ROWS, 512), F32)
    for bit in range(4):
        total = total + jnp.dot(
            rows_ref[place_ref[3] ^ bit], weights[bit][...], preferred_element_type=F32
        )
    keep_ref[...] = total[:, :256]
    send_ref[...] = total[:, 256:]


def project(place, rows, weights):
    return pl.pallas_call(
        project_kernel,
        in_specs=[SMEM] + [VMEM] * 5,
        out_specs=[VMEM] * 2,
        out_shape=[jax.ShapeDtypeStruct((ROWS, 256), F32)] * 2,
        compiler_params=pltpu.CompilerParams(vmem_limit_bytes=16 * 1024 * 1024),
    )(place, rows, *weights)


def shards(query_rows, key_rows, value_rows, out_weight):
    q, k, v = (rows.reshape(1, ROWS, DIM) for rows in (query_rows, key_rows, value_rows))
    ctx, head = lax.axis_index("ctx"), lax.axis_index("head")
    place = jnp.stack(
        [ctx % 4, ctx // 4, head // 8, head // 2 % 4, head % 2]
    ).astype(jnp.int32)
    pair, q, out_weight = lax.optimization_barrier((jnp.concatenate([k, v]), q, out_weight))
    far = ctx_send(pair, dza=1)
    q_far = ctx_send(q, dzb=2)
    near_pieces = [pair] + [ctx_send(pair, dy=bits) for bits in (1, 2, 3)]
    queries = [q, q_far, ctx_send(jnp.concatenate([q, q_far]), dzb=1)]
    parts = weight_parts(place, out_weight)
    weights = [parts[0]] + [head_send(parts[bits], dx=bits) for bits in (1, 2, 3)]
    far_pieces = [far] + [ctx_send(far, dy=bits) for bits in (1, 2, 3)]

    expo_near, stats_near = first_scores(queries, near_pieces)
    far_pieces, weights, stats_near = lax.optimization_barrier((far_pieces, weights, stats_near))
    expo_far, stats_far, stats = second_scores(place, queries, far_pieces, stats_near)
    expos = (expo_near, expo_far)
    factor, sums = columns(place, expos, (stats_near, stats_far), swap(stats, "ctx", LINE))
    attended = attend(place, expos, factor, near_pieces + far_pieces, swap(sums, "ctx", PLANE))
    whole = jnp.sum(swap(attended, "ctx", LINE).astype(F32), axis=0).astype(BF16)
    rows = swap(jnp.broadcast_to(whole, (4, ROWS, DIM)), "head", ROW)
    keep, send = project(place, rows, weights)
    both = keep + head_send(send, dcore=1)
    far = head_send(both[:, 128:].astype(BF16), dzh=1)
    return (both[:, :128] + far.astype(F32)).astype(BF16)


def solution(mesh):
    placed = (
        P("ctx", "head", None),
        P("ctx", "head", None),
        P("ctx", "head", None),
        P("head", None),
    )
    return jax.shard_map(
        shards, mesh=mesh, in_specs=placed, out_specs=P("ctx", "head"), check_vma=False
    )
```

```python
import functools
import math

import jax
import jax.numpy as jnp
from jax import lax
from jax.experimental import pallas as pl
from jax.experimental.pallas import tpu as pltpu
from jax.sharding import PartitionSpec as P

F32 = jnp.float32
BF16 = jnp.bfloat16
ROWS = 384
DIM = 128
QB = 4
KB = 8
HALF = 4 * ROWS
KEY_BITS = ((0, 2, 4, 6), (1, 3, 5, 7))
QUERY_BITS = (0, 2, 1, 3)
GROUPS = ROWS // 128
SUB = 128
EXP_SCALE = DIM ** -0.5 * math.log2(math.e)
LIFT = 2.0 ** 20
NT = (((1,), (1,)), ((), ()))
VMEM = pl.BlockSpec(memory_space=pltpu.VMEM)


def ctx_send(value, dy=0, dza=0, dzb=0):
    step = dy * 8 + dza * 4 + dzb
    return lax.ppermute(value, "ctx", [(i, i ^ step) for i in range(32)])


def head_send(value, dzh=0, dx=0, dcore=0):
    step = dzh * 8 + dx * 2 + dcore
    return lax.ppermute(value, "head", [(i, i ^ step) for i in range(16)])


LINE = [[y * 8 + za * 4 + zb for zb in range(4)] for y in range(4) for za in range(2)]
PLANE = [[y * 8 + za * 4 + zb for y in range(4) for za in range(2)] for zb in range(4)]
ROW = [[zh * 8 + x * 2 + core for x in range(4)] for zh in range(2) for core in range(2)]


def swap(value, axis, groups):
    return lax.all_to_all(value, axis, 0, 0, axis_index_groups=groups, tiled=True)


def columns_to_rows(columns):
    lane = lax.broadcasted_iota(jnp.int32, (128, 128), 1)
    square = jnp.zeros((128, 128), F32)
    for at, column in enumerate(columns):
        square = jnp.where(lane == at, column, square)
    return square.T[:8]


def rows_to_columns(rows):
    return jnp.concatenate([rows] * 16, axis=0).T


def gather_queries(u, q_refs, q_all):
    @pl.when(u == 0)
    def _():
        for at in range(QB):
            q_all[at] = q_refs[at // 2][at % 2]


def half_scores(u, q_all, kv_refs, e_ref, s_ref):
    peaks, totals = [], []
    for sub in range(GROUPS):
        q = q_all[u, sub * SUB : (sub + 1) * SUB, :]
        top = jnp.full((SUB, 128), -jnp.inf, F32)
        for b in range(4):
            s = lax.dot_general(q, kv_refs[b][0], NT, preferred_element_type=F32)
            s_ref[sub, :, b * ROWS : (b + 1) * ROWS] = s
            for g in range(GROUPS):
                top = jnp.maximum(top, s[:, g * 128 : (g + 1) * 128])
        peak = jnp.max(top, axis=1, keepdims=True)
        total = jnp.zeros((SUB, 128), F32)
        for b in range(4 * GROUPS):
            e = jnp.exp2((s_ref[sub, :, b * 128 : (b + 1) * 128] - peak) * EXP_SCALE)
            total = total + e
            e_ref[sub * SUB : (sub + 1) * SUB, b * 128 : (b + 1) * 128] = e.astype(BF16)
        peaks.append(peak)
        totals.append(jnp.sum(total, axis=1, keepdims=True))
    return columns_to_rows(peaks + totals)


def first_score_kernel(*refs):
    q_refs, kv_refs, (e_ref, stat_ref, q_all, s_ref) = refs[:2], refs[2:6], refs[6:]
    u = pl.program_id(0)
    gather_queries(u, q_refs, q_all)
    stat_ref[u] = half_scores(u, q_all, kv_refs, e_ref, s_ref)


def combine(a, b):
    peak = jnp.maximum(a[:GROUPS], b[:GROUPS])
    total = a[GROUPS : 2 * GROUPS] * jnp.exp2((a[:GROUPS] - peak) * EXP_SCALE)
    total = total + b[GROUPS : 2 * GROUPS] * jnp.exp2((b[:GROUPS] - peak) * EXP_SCALE)
    return jnp.concatenate([peak, total, jnp.zeros((8 - 2 * GROUPS, 128), F32)], axis=0)


def second_score_kernel(place_ref, *refs):
    q_refs, kv_refs, first_ref = refs[:2], refs[2:6], refs[6]
    e_ref, stat_ref, both_ref, q_all, s_ref = refs[7:]
    u = pl.program_id(0)
    gather_queries(u, q_refs, q_all)
    rows = half_scores(u, q_all, kv_refs, e_ref, s_ref)
    stat_ref[u] = rows
    rows = combine(first_ref[u], rows)
    at = place_ref[0] ^ ((u % 2) * 2 + u // 2)
    for to in range(QB):
        both_ref[to, at] = rows


SMEM = pl.BlockSpec(memory_space=pltpu.SMEM)
EXPO = pl.BlockSpec((ROWS, HALF), lambda u: (u, 0))
SCORE = dict(
    grid=(QB,),
    scratch_shapes=[pltpu.VMEM((QB, ROWS, DIM), BF16), pltpu.VMEM((GROUPS, SUB, HALF), F32)],
    compiler_params=pltpu.CompilerParams(vmem_limit_bytes=16 * 1024 * 1024),
)
EXPO_TYPE = jax.ShapeDtypeStruct((QB * ROWS, HALF), BF16)
STAT_TYPE = jax.ShapeDtypeStruct((QB, 8, 128), F32)


def first_scores(queries, pieces):
    return pl.pallas_call(
        first_score_kernel,
        in_specs=[VMEM] * 6,
        out_specs=[EXPO, VMEM],
        out_shape=[EXPO_TYPE, STAT_TYPE],
        **SCORE,
    )(*queries, *pieces)


def second_scores(place, queries, pieces, stats):
    return pl.pallas_call(
        second_score_kernel,
        in_specs=[SMEM] + [VMEM] * 7,
        out_specs=[EXPO, VMEM, VMEM],
        out_shape=[EXPO_TYPE, STAT_TYPE, jax.ShapeDtypeStruct((QB, QB, 8, 128), F32)],
        **SCORE,
    )(place, *queries, *pieces, stats)


def column_kernel(
    place_ref, e0_ref, e1_ref, stat0_ref, stat1_ref, all_ref, factor_ref, column_ref, sum_ref
):
    u = pl.program_id(0)

    @pl.when(u == 0)
    def _():
        for block in range(QB):
            at = place_ref[0] ^ QUERY_BITS[block]
            whole = functools.reduce(combine, [all_ref[j, at] for j in range(QB)])
            for half, stat_ref in enumerate((stat0_ref, stat1_ref)):
                mine = stat_ref[block]
                factor = jnp.exp2((mine[:GROUPS] - whole[:GROUPS]) * EXP_SCALE)
                factor = factor / whole[GROUPS : 2 * GROUPS]
                factor_ref[half, block] = jnp.concatenate(
                    [factor, jnp.zeros((8 - GROUPS, 128), F32)], axis=0
                )
        sum_ref[...] = jnp.zeros_like(sum_ref)

    at = lax.broadcasted_iota(jnp.int32, (16, ROWS), 0)
    for half, e_ref in enumerate((e0_ref, e1_ref)):
        mine = factor_ref[half, u]
        row = jnp.concatenate([mine[g : g + 1] for g in range(GROUPS)], axis=1)
        high = row.astype(BF16).astype(F32)
        left = jnp.where(at == 0, high, jnp.where(at == 1, row - high, 0.0)).astype(BF16)
        sum_ref[half] += jnp.dot(left, e_ref[...], preferred_element_type=F32)

    @pl.when(u == QB - 1)
    def _():
        for half in range(2):
            whole = sum_ref[half, 0:1] + sum_ref[half, 1:2]
            for b in range(4):
                row = whole[:, b * ROWS : (b + 1) * ROWS]
                column_ref[0, pl.ds(place_ref[1] ^ KEY_BITS[half][b], 1)] = row
        for to in range(1, KB):
            column_ref[to] = column_ref[0]


def columns(place, expos, stats, all_stats):
    return pl.pallas_call(
        column_kernel,
        grid=(QB,),
        in_specs=[SMEM, EXPO, EXPO, VMEM, VMEM, VMEM],
        out_specs=[VMEM, VMEM],
        out_shape=[
            jax.ShapeDtypeStruct((2, QB, 8, 128), F32),
            jax.ShapeDtypeStruct((KB, KB, ROWS), F32),
        ],
        scratch_shapes=[pltpu.VMEM((2, 16, HALF), F32)],
        compiler_params=pltpu.CompilerParams(vmem_limit_bytes=16 * 1024 * 1024),
    )(place, *expos, *stats, all_stats)


def value_kernel(place_ref, e0_ref, e1_ref, factor_ref, *refs):
    kv_refs, (sums_ref, out_ref, scaled, inverse) = refs[:KB], refs[KB:]
    u = pl.program_id(0)

    @pl.when(u == 0)
    def _():
        inverse[...] = (1.0 / LIFT) / functools.reduce(
            jnp.add, [sums_ref[j] for j in range(KB)]
        )
        bits = KEY_BITS[0] + KEY_BITS[1]
        rows = jnp.concatenate(
            [inverse[pl.ds(place_ref[1] ^ bit, 1)] for bit in bits], axis=0
        )
        for g in range(GROUPS):
            column = rows_to_columns(rows[:, g * 128 : (g + 1) * 128])
            for b in range(KB):
                part = kv_refs[b][1, g * 128 : (g + 1) * 128, :].astype(F32)
                scaled[b * ROWS + g * 128 : b * ROWS + (g + 1) * 128, :] = (
                    part * column[:, b : b + 1]
                ).astype(BF16)

    parts = []
    for half, e_ref in enumerate((e0_ref, e1_ref)):
        part = jnp.dot(
            e_ref[...], scaled[half * HALF : (half + 1) * HALF], preferred_element_type=F32
        )
        parts.append((part, rows_to_columns(factor_ref[half, u]) * LIFT))
    at = place_ref[0] ^ ((u % 2) * 2 + u // 2)
    for g in range(GROUPS):
        rows = slice(g * 128, (g + 1) * 128)
        out_ref[at, rows, :] = sum(
            part[rows] * column[:, g : g + 1] for part, column in parts
        ).astype(BF16)


def attend(place, expos, factor, pieces, sums):
    return pl.pallas_call(
        value_kernel,
        grid=(QB,),
        in_specs=[SMEM, EXPO, EXPO] + [VMEM] * (KB + 2),
        out_specs=VMEM,
        out_shape=jax.ShapeDtypeStruct((QB, ROWS, DIM), BF16),
        scratch_shapes=[pltpu.VMEM((2 * HALF, DIM), BF16), pltpu.VMEM((KB, ROWS), F32)],
        compiler_params=pltpu.CompilerParams(vmem_limit_bytes=16 * 1024 * 1024),
    )(place, *expos, factor, *pieces, sums)


def project_kernel(place_ref, own_ref, other_ref, w0_ref, w1_ref, out_ref, w_ref):
    zh, core = place_ref[2], place_ref[4]
    for x in range(4):
        for dzh in range(2):
            head = (zh ^ dzh) * 8 + x * 2 + core
            lanes = pl.ds(pl.multiple_of(head * 128, 128), 128)
            at = slice((x * 2 + dzh) * 128, (x * 2 + dzh + 1) * 128)
            w_ref[:DIM, at] = w0_ref[:, lanes]
            w_ref[DIM:, at] = w1_ref[:, lanes]
    rows = jnp.concatenate([own_ref[...], other_ref[...]], axis=1)
    for x in range(4):
        out_ref[x] = jnp.dot(
            rows, w_ref[:, x * 256 : (x + 1) * 256], preferred_element_type=F32
        ).astype(BF16)


def project(place, own, other, w_own, w_other):
    return pl.pallas_call(
        project_kernel,
        in_specs=[SMEM] + [VMEM] * 4,
        out_specs=VMEM,
        out_shape=jax.ShapeDtypeStruct((4, ROWS, 256), BF16),
        scratch_shapes=[pltpu.VMEM((2 * DIM, 1024), BF16)],
        compiler_params=pltpu.CompilerParams(vmem_limit_bytes=16 * 1024 * 1024),
    )(place, own, other, w_own, w_other)


def query_pair_kernel(a_ref, b_ref, out_ref):
    out_ref[0] = a_ref[0]
    out_ref[1] = b_ref[0]


def query_pair(a, b):
    return pl.pallas_call(
        query_pair_kernel,
        in_specs=[VMEM] * 2,
        out_specs=VMEM,
        out_shape=jax.ShapeDtypeStruct((2, ROWS, DIM), BF16),
        compiler_params=pltpu.CompilerParams(vmem_limit_bytes=8 * 1024 * 1024),
        cost_estimate=pl.CostEstimate(flops=2 * 10**10, bytes_accessed=10**6, transcendentals=0),
    )(a, b)


def shards(query_rows, key_rows, value_rows, out_weight):
    q, k, v = (rows.reshape(1, ROWS, DIM) for rows in (query_rows, key_rows, value_rows))
    ctx, head = lax.axis_index("ctx"), lax.axis_index("head")
    place = jnp.stack(
        [ctx % 4, ctx // 4, head // 8, head // 2 % 4, head % 2]
    ).astype(jnp.int32)
    pair, q = lax.optimization_barrier((jnp.concatenate([k, v]), q))
    far = ctx_send(pair, dza=1)
    q_two = query_pair(q, ctx_send(q, dzb=2))
    near_pieces = [pair] + [ctx_send(pair, dy=bits) for bits in (1, 2, 3)]
    queries = [q_two, ctx_send(q_two, dzb=1)]
    far_pieces = [far] + [ctx_send(far, dy=bits) for bits in (1, 2, 3)]

    expo_near, stats_near = first_scores(queries, near_pieces)
    w_other = head_send(out_weight, dcore=1)
    far_pieces, w_other, stats_near = lax.optimization_barrier((far_pieces, w_other, stats_near))
    expo_far, stats_far, stats = second_scores(place, queries, far_pieces, stats_near)
    expos = (expo_near, expo_far)
    factor, sums = columns(place, expos, (stats_near, stats_far), swap(stats, "ctx", LINE))
    attended = attend(place, expos, factor, near_pieces + far_pieces, swap(sums, "ctx", PLANE))
    whole = jnp.sum(swap(attended, "ctx", LINE).astype(F32), axis=0).astype(BF16)
    parts = project(place, whole, head_send(whole, dcore=1), out_weight, w_other)
    both = jnp.sum(swap(parts, "head", ROW).astype(F32), axis=0)
    far = head_send(both[:, 128:].astype(BF16), dzh=1)
    return (both[:, :128] + far.astype(F32)).astype(BF16)


def solution(mesh):
    placed = (
        P("ctx", "head", None),
        P("ctx", "head", None),
        P("ctx", "head", None),
        P("head", None),
    )
    return jax.shard_map(
        shards, mesh=mesh, in_specs=placed, out_specs=P("ctx", "head"), check_vma=False
    )
```

```python
import functools
import math

import jax
import jax.numpy as jnp
from jax import lax
from jax.experimental import pallas as pl
from jax.experimental.pallas import tpu as pltpu
from jax.sharding import PartitionSpec as P

F32 = jnp.float32
BF16 = jnp.bfloat16
ROWS = 384
DIM = 128
QB = 4
KB = 8
HALF = 4 * ROWS
KEY_BITS = ((0, 2, 4, 6), (1, 3, 5, 7))
QUERY_BITS = (0, 2, 1, 3)
GROUPS = ROWS // 128
SUB = 128
EXP_SCALE = DIM ** -0.5 * math.log2(math.e)
LIFT = 2.0 ** 20
NT = (((1,), (1,)), ((), ()))
VMEM = pl.BlockSpec(memory_space=pltpu.VMEM)


def ctx_send(value, dy=0, dza=0, dzb=0):
    step = dy * 8 + dza * 4 + dzb
    return lax.ppermute(value, "ctx", [(i, i ^ step) for i in range(32)])


def head_send(value, dzh=0, dx=0, dcore=0):
    step = dzh * 8 + dx * 2 + dcore
    return lax.ppermute(value, "head", [(i, i ^ step) for i in range(16)])


LINE = [[y * 8 + za * 4 + zb for zb in range(4)] for y in range(4) for za in range(2)]
PLANE = [[y * 8 + za * 4 + zb for y in range(4) for za in range(2)] for zb in range(4)]
ROW = [[zh * 8 + x * 2 + core for x in range(4)] for zh in range(2) for core in range(2)]


def swap(value, axis, groups):
    return lax.all_to_all(value, axis, 0, 0, axis_index_groups=groups, tiled=True)


def columns_to_rows(columns):
    lane = lax.broadcasted_iota(jnp.int32, (128, 128), 1)
    square = jnp.zeros((128, 128), F32)
    for at, column in enumerate(columns):
        square = jnp.where(lane == at, column, square)
    return square.T[:8]


def rows_to_columns(rows):
    return jnp.concatenate([rows] * 16, axis=0).T


def gather_queries(u, q_refs, q_all):
    @pl.when(u == 0)
    def _():
        for at in range(QB):
            q_all[at] = q_refs[at // 2][at % 2]


def half_scores(u, q_all, kv_refs, e_ref, s_ref):
    peaks, totals = [], []
    for sub in range(GROUPS):
        q = q_all[u, sub * SUB : (sub + 1) * SUB, :]
        top = jnp.full((SUB, 128), -jnp.inf, F32)
        for b in range(4):
            s = lax.dot_general(q, kv_refs[b][0], NT, preferred_element_type=F32)
            s_ref[sub, :, b * ROWS : (b + 1) * ROWS] = s
            for g in range(GROUPS):
                top = jnp.maximum(top, s[:, g * 128 : (g + 1) * 128])
        peak = jnp.max(top, axis=1, keepdims=True)
        total = jnp.zeros((SUB, 128), F32)
        for b in range(4 * GROUPS):
            e = jnp.exp2((s_ref[sub, :, b * 128 : (b + 1) * 128] - peak) * EXP_SCALE)
            total = total + e
            e_ref[sub * SUB : (sub + 1) * SUB, b * 128 : (b + 1) * 128] = e.astype(BF16)
        peaks.append(peak)
        totals.append(jnp.sum(total, axis=1, keepdims=True))
    return columns_to_rows(peaks + totals)


def first_score_kernel(*refs):
    q_refs, kv_refs, (e_ref, stat_ref, q_all, s_ref) = refs[:2], refs[2:6], refs[6:]
    u = pl.program_id(0)
    gather_queries(u, q_refs, q_all)
    stat_ref[u] = half_scores(u, q_all, kv_refs, e_ref, s_ref)


def combine(a, b):
    peak = jnp.maximum(a[:GROUPS], b[:GROUPS])
    total = a[GROUPS : 2 * GROUPS] * jnp.exp2((a[:GROUPS] - peak) * EXP_SCALE)
    total = total + b[GROUPS : 2 * GROUPS] * jnp.exp2((b[:GROUPS] - peak) * EXP_SCALE)
    return jnp.concatenate([peak, total, jnp.zeros((8 - 2 * GROUPS, 128), F32)], axis=0)


def second_score_kernel(place_ref, *refs):
    q_refs, kv_refs, first_ref = refs[:2], refs[2:6], refs[6]
    e_ref, stat_ref, both_ref, q_all, s_ref = refs[7:]
    u = pl.program_id(0)
    gather_queries(u, q_refs, q_all)
    rows = half_scores(u, q_all, kv_refs, e_ref, s_ref)
    stat_ref[u] = rows
    rows = combine(first_ref[u], rows)
    at = place_ref[0] ^ ((u % 2) * 2 + u // 2)
    for to in range(QB):
        both_ref[to, at] = rows


SMEM = pl.BlockSpec(memory_space=pltpu.SMEM)
EXPO = pl.BlockSpec((ROWS, HALF), lambda u: (u, 0))
SCORE = dict(
    grid=(QB,),
    scratch_shapes=[pltpu.VMEM((QB, ROWS, DIM), BF16), pltpu.VMEM((GROUPS, SUB, HALF), F32)],
    compiler_params=pltpu.CompilerParams(vmem_limit_bytes=16 * 1024 * 1024),
)
EXPO_TYPE = jax.ShapeDtypeStruct((QB * ROWS, HALF), BF16)
STAT_TYPE = jax.ShapeDtypeStruct((QB, 8, 128), F32)


def first_scores(queries, pieces):
    return pl.pallas_call(
        first_score_kernel,
        in_specs=[VMEM] * 6,
        out_specs=[EXPO, VMEM],
        out_shape=[EXPO_TYPE, STAT_TYPE],
        **SCORE,
    )(*queries, *pieces)


def second_scores(place, queries, pieces, stats):
    return pl.pallas_call(
        second_score_kernel,
        in_specs=[SMEM] + [VMEM] * 7,
        out_specs=[EXPO, VMEM, VMEM],
        out_shape=[EXPO_TYPE, STAT_TYPE, jax.ShapeDtypeStruct((QB, QB, 8, 128), F32)],
        **SCORE,
    )(place, *queries, *pieces, stats)


def column_kernel(
    place_ref, e0_ref, e1_ref, stat0_ref, stat1_ref, all_ref, factor_ref, column_ref, sum_ref
):
    u = pl.program_id(0)

    @pl.when(u == 0)
    def _():
        for block in range(QB):
            at = place_ref[0] ^ QUERY_BITS[block]
            whole = functools.reduce(combine, [all_ref[j, at] for j in range(QB)])
            for half, stat_ref in enumerate((stat0_ref, stat1_ref)):
                mine = stat_ref[block]
                factor = jnp.exp2((mine[:GROUPS] - whole[:GROUPS]) * EXP_SCALE)
                factor = factor / whole[GROUPS : 2 * GROUPS]
                factor_ref[half, block] = jnp.concatenate(
                    [factor, jnp.zeros((8 - GROUPS, 128), F32)], axis=0
                )
        sum_ref[...] = jnp.zeros_like(sum_ref)

    at = lax.broadcasted_iota(jnp.int32, (16, ROWS), 0)
    for half, e_ref in enumerate((e0_ref, e1_ref)):
        mine = factor_ref[half, u]
        row = jnp.concatenate([mine[g : g + 1] for g in range(GROUPS)], axis=1)
        high = row.astype(BF16).astype(F32)
        left = jnp.where(at == 0, high, jnp.where(at == 1, row - high, 0.0)).astype(BF16)
        sum_ref[half] += jnp.dot(left, e_ref[...], preferred_element_type=F32)

    @pl.when(u == QB - 1)
    def _():
        for half in range(2):
            whole = sum_ref[half, 0:1] + sum_ref[half, 1:2]
            for b in range(4):
                row = whole[:, b * ROWS : (b + 1) * ROWS]
                column_ref[0, pl.ds(place_ref[1] ^ KEY_BITS[half][b], 1)] = row
        for to in range(1, KB):
            column_ref[to] = column_ref[0]


def columns(place, expos, stats, all_stats):
    return pl.pallas_call(
        column_kernel,
        grid=(QB,),
        in_specs=[SMEM, EXPO, EXPO, VMEM, VMEM, VMEM],
        out_specs=[VMEM, VMEM],
        out_shape=[
            jax.ShapeDtypeStruct((2, QB, 8, 128), F32),
            jax.ShapeDtypeStruct((KB, KB, ROWS), F32),
        ],
        scratch_shapes=[pltpu.VMEM((2, 16, HALF), F32)],
        compiler_params=pltpu.CompilerParams(vmem_limit_bytes=16 * 1024 * 1024),
    )(place, *expos, *stats, all_stats)


def value_kernel(place_ref, e0_ref, e1_ref, factor_ref, *refs):
    kv_refs, (sums_ref, out_ref, scaled, inverse) = refs[:KB], refs[KB:]
    u = pl.program_id(0)

    @pl.when(u == 0)
    def _():
        inverse[...] = (1.0 / LIFT) / functools.reduce(
            jnp.add, [sums_ref[j] for j in range(KB)]
        )
        bits = KEY_BITS[0] + KEY_BITS[1]
        rows = jnp.concatenate(
            [inverse[pl.ds(place_ref[1] ^ bit, 1)] for bit in bits], axis=0
        )
        for g in range(GROUPS):
            column = rows_to_columns(rows[:, g * 128 : (g + 1) * 128])
            for b in range(KB):
                part = kv_refs[b][1, g * 128 : (g + 1) * 128, :].astype(F32)
                scaled[b * ROWS + g * 128 : b * ROWS + (g + 1) * 128, :] = (
                    part * column[:, b : b + 1]
                ).astype(BF16)

    parts = []
    for half, e_ref in enumerate((e0_ref, e1_ref)):
        part = jnp.dot(
            e_ref[...], scaled[half * HALF : (half + 1) * HALF], preferred_element_type=F32
        )
        parts.append((part, rows_to_columns(factor_ref[half, u]) * LIFT))
    at = place_ref[0] ^ ((u % 2) * 2 + u // 2)
    for g in range(GROUPS):
        rows = slice(g * 128, (g + 1) * 128)
        out_ref[at, rows, :] = sum(
            part[rows] * column[:, g : g + 1] for part, column in parts
        ).astype(BF16)


def attend(place, expos, factor, pieces, sums):
    return pl.pallas_call(
        value_kernel,
        grid=(QB,),
        in_specs=[SMEM, EXPO, EXPO] + [VMEM] * (KB + 2),
        out_specs=VMEM,
        out_shape=jax.ShapeDtypeStruct((QB, ROWS, DIM), BF16),
        scratch_shapes=[pltpu.VMEM((2 * HALF, DIM), BF16), pltpu.VMEM((KB, ROWS), F32)],
        compiler_params=pltpu.CompilerParams(vmem_limit_bytes=16 * 1024 * 1024),
    )(place, *expos, factor, *pieces, sums)


def project_kernel(place_ref, own_ref, other_ref, w0_ref, w1_ref, near_ref, far_ref, w_ref):
    zh, core = place_ref[2], place_ref[4]
    for x in range(4):
        for dzh in range(2):
            head = (zh ^ dzh) * 8 + x * 2 + core
            lanes = pl.ds(pl.multiple_of(head * 128, 128), 128)
            at = slice((x * 2 + dzh) * 128, (x * 2 + dzh + 1) * 128)
            w_ref[:DIM, at] = w0_ref[:, lanes]
            w_ref[DIM:, at] = w1_ref[:, lanes]
    rows = jnp.concatenate([own_ref[...], other_ref[...]], axis=1)
    for x in range(4):
        part = jnp.dot(rows, w_ref[:, x * 256 : (x + 1) * 256], preferred_element_type=F32)
        near_ref[x] = part[:, :128].astype(BF16)
        far_ref[x] = part[:, 128:].astype(BF16)


def project(place, own, other, w_own, w_other):
    return pl.pallas_call(
        project_kernel,
        in_specs=[SMEM] + [VMEM] * 4,
        out_specs=[VMEM] * 2,
        out_shape=[jax.ShapeDtypeStruct((4, ROWS, 128), BF16)] * 2,
        scratch_shapes=[pltpu.VMEM((2 * DIM, 1024), BF16)],
        compiler_params=pltpu.CompilerParams(vmem_limit_bytes=16 * 1024 * 1024),
    )(place, own, other, w_own, w_other)


def query_pair_kernel(a_ref, b_ref, out_ref):
    out_ref[0] = a_ref[0]
    out_ref[1] = b_ref[0]


def query_pair(a, b):
    return pl.pallas_call(
        query_pair_kernel,
        in_specs=[VMEM] * 2,
        out_specs=VMEM,
        out_shape=jax.ShapeDtypeStruct((2, ROWS, DIM), BF16),
        compiler_params=pltpu.CompilerParams(vmem_limit_bytes=8 * 1024 * 1024),
        cost_estimate=pl.CostEstimate(flops=2 * 10**10, bytes_accessed=10**6, transcendentals=0),
    )(a, b)


def shards(query_rows, key_rows, value_rows, out_weight):
    q, k, v = (rows.reshape(1, ROWS, DIM) for rows in (query_rows, key_rows, value_rows))
    ctx, head = lax.axis_index("ctx"), lax.axis_index("head")
    place = jnp.stack(
        [ctx % 4, ctx // 4, head // 8, head // 2 % 4, head % 2]
    ).astype(jnp.int32)
    pair, q = lax.optimization_barrier((jnp.concatenate([k, v]), q))
    far = ctx_send(pair, dza=1)
    q_two = query_pair(q, ctx_send(q, dzb=2))
    near_pieces = [pair] + [ctx_send(pair, dy=bits) for bits in (1, 2, 3)]
    queries = [q_two, ctx_send(q_two, dzb=1)]
    far_pieces = [far] + [ctx_send(far, dy=bits) for bits in (1, 2, 3)]

    expo_near, stats_near = first_scores(queries, near_pieces)
    w_other = head_send(out_weight, dcore=1)
    far_pieces, w_other, stats_near = lax.optimization_barrier((far_pieces, w_other, stats_near))
    expo_far, stats_far, stats = second_scores(place, queries, far_pieces, stats_near)
    expos = (expo_near, expo_far)
    factor, sums = columns(place, expos, (stats_near, stats_far), swap(stats, "ctx", LINE))
    attended = attend(place, expos, factor, near_pieces + far_pieces, swap(sums, "ctx", PLANE))
    whole = jnp.sum(swap(attended, "ctx", LINE).astype(F32), axis=0).astype(BF16)
    near, far = project(place, whole, head_send(whole, dcore=1), out_weight, w_other)
    far = jnp.sum(swap(far, "head", ROW).astype(F32), axis=0).astype(BF16)
    near, far = lax.optimization_barrier((near, far))
    far = head_send(far, dzh=1)
    near = jnp.sum(swap(near, "head", ROW).astype(F32), axis=0)
    return (near + far.astype(F32)).astype(BF16)


def solution(mesh):
    placed = (
        P("ctx", "head", None),
        P("ctx", "head", None),
        P("ctx", "head", None),
        P("head", None),
    )
    return jax.shard_map(
        shards, mesh=mesh, in_specs=placed, out_specs=P("ctx", "head"), check_vma=False
    )
```

```python
import functools
import math

import jax
import jax.numpy as jnp
from jax import lax
from jax.experimental import pallas as pl
from jax.experimental.pallas import tpu as pltpu
from jax.sharding import PartitionSpec as P

F32 = jnp.float32
BF16 = jnp.bfloat16
ROWS = 384
DIM = 128
QB = 4
KB = 8
HALF = 4 * ROWS
KEY_BITS = ((0, 2, 4, 6), (1, 3, 5, 7))
QUERY_BITS = (0, 2, 1, 3)
GROUPS = ROWS // 128
SUB = 128
EXP_SCALE = DIM ** -0.5 * math.log2(math.e)
LIFT = 2.0 ** 20
NT = (((1,), (1,)), ((), ()))
VMEM = pl.BlockSpec(memory_space=pltpu.VMEM)


def ctx_send(value, dy=0, dza=0, dzb=0):
    step = dy * 8 + dza * 4 + dzb
    return lax.ppermute(value, "ctx", [(i, i ^ step) for i in range(32)])


def head_send(value, dzh=0, dx=0, dcore=0):
    step = dzh * 8 + dx * 2 + dcore
    return lax.ppermute(value, "head", [(i, i ^ step) for i in range(16)])


LINE = [[y * 8 + za * 4 + zb for zb in range(4)] for y in range(4) for za in range(2)]
PLANE = [[y * 8 + za * 4 + zb for y in range(4) for za in range(2)] for zb in range(4)]
ROW = [[zh * 8 + x * 2 + core for x in range(4)] for zh in range(2) for core in range(2)]


def swap(value, axis, groups):
    return lax.all_to_all(value, axis, 0, 0, axis_index_groups=groups, tiled=True)


def columns_to_rows(columns):
    lane = lax.broadcasted_iota(jnp.int32, (128, 128), 1)
    square = jnp.zeros((128, 128), F32)
    for at, column in enumerate(columns):
        square = jnp.where(lane == at, column, square)
    return square.T[:8]


def rows_to_columns(rows):
    return jnp.concatenate([rows] * 16, axis=0).T


def gather_queries(u, q_refs, q_all):
    @pl.when(u == 0)
    def _():
        for at in range(QB):
            q_all[at] = q_refs[at // 2][at % 2]


def half_scores(u, q_all, kv_refs, e_ref, s_ref):
    peaks, totals = [], []
    for sub in range(GROUPS):
        q = q_all[u, sub * SUB : (sub + 1) * SUB, :]
        top = jnp.full((SUB, 128), -jnp.inf, F32)
        for b in range(4):
            s = lax.dot_general(q, kv_refs[b][0], NT, preferred_element_type=F32)
            s_ref[sub, :, b * ROWS : (b + 1) * ROWS] = s
            for g in range(GROUPS):
                top = jnp.maximum(top, s[:, g * 128 : (g + 1) * 128])
        peak = jnp.max(top, axis=1, keepdims=True)
        total = jnp.zeros((SUB, 128), F32)
        for b in range(4 * GROUPS):
            e = jnp.exp2((s_ref[sub, :, b * 128 : (b + 1) * 128] - peak) * EXP_SCALE)
            total = total + e
            e_ref[sub * SUB : (sub + 1) * SUB, b * 128 : (b + 1) * 128] = e.astype(BF16)
        peaks.append(peak)
        totals.append(jnp.sum(total, axis=1, keepdims=True))
    return columns_to_rows(peaks + totals)


def first_score_kernel(*refs):
    q_refs, kv_refs, (e_ref, stat_ref, q_all, s_ref) = refs[:2], refs[2:6], refs[6:]
    u = pl.program_id(0)
    gather_queries(u, q_refs, q_all)
    stat_ref[u] = half_scores(u, q_all, kv_refs, e_ref, s_ref)


def combine(a, b):
    peak = jnp.maximum(a[:GROUPS], b[:GROUPS])
    total = a[GROUPS : 2 * GROUPS] * jnp.exp2((a[:GROUPS] - peak) * EXP_SCALE)
    total = total + b[GROUPS : 2 * GROUPS] * jnp.exp2((b[:GROUPS] - peak) * EXP_SCALE)
    return jnp.concatenate([peak, total, jnp.zeros((8 - 2 * GROUPS, 128), F32)], axis=0)


def second_score_kernel(place_ref, *refs):
    q_refs, kv_refs, first_ref = refs[:2], refs[2:6], refs[6]
    e_ref, stat_ref, both_ref, q_all, s_ref = refs[7:]
    u = pl.program_id(0)
    gather_queries(u, q_refs, q_all)
    rows = half_scores(u, q_all, kv_refs, e_ref, s_ref)
    stat_ref[u] = rows
    rows = combine(first_ref[u], rows)
    at = place_ref[0] ^ ((u % 2) * 2 + u // 2)
    for to in range(QB):
        both_ref[to, at] = rows


SMEM = pl.BlockSpec(memory_space=pltpu.SMEM)
EXPO = pl.BlockSpec((ROWS, HALF), lambda u: (u, 0))
SCORE = dict(
    grid=(QB,),
    scratch_shapes=[pltpu.VMEM((QB, ROWS, DIM), BF16), pltpu.VMEM((GROUPS, SUB, HALF), F32)],
    compiler_params=pltpu.CompilerParams(vmem_limit_bytes=16 * 1024 * 1024),
)
EXPO_TYPE = jax.ShapeDtypeStruct((QB * ROWS, HALF), BF16)
STAT_TYPE = jax.ShapeDtypeStruct((QB, 8, 128), F32)


def first_scores(queries, pieces):
    return pl.pallas_call(
        first_score_kernel,
        in_specs=[VMEM] * 6,
        out_specs=[EXPO, VMEM],
        out_shape=[EXPO_TYPE, STAT_TYPE],
        **SCORE,
    )(*queries, *pieces)


def second_scores(place, queries, pieces, stats):
    return pl.pallas_call(
        second_score_kernel,
        in_specs=[SMEM] + [VMEM] * 7,
        out_specs=[EXPO, VMEM, VMEM],
        out_shape=[EXPO_TYPE, STAT_TYPE, jax.ShapeDtypeStruct((QB, QB, 8, 128), F32)],
        **SCORE,
    )(place, *queries, *pieces, stats)


def column_kernel(
    place_ref, e0_ref, e1_ref, stat0_ref, stat1_ref, all_ref, factor_ref, column_ref, sum_ref
):
    u = pl.program_id(0)

    @pl.when(u == 0)
    def _():
        for block in range(QB):
            at = place_ref[0] ^ QUERY_BITS[block]
            whole = functools.reduce(combine, [all_ref[j, at] for j in range(QB)])
            for half, stat_ref in enumerate((stat0_ref, stat1_ref)):
                mine = stat_ref[block]
                factor = jnp.exp2((mine[:GROUPS] - whole[:GROUPS]) * EXP_SCALE)
                factor = factor / whole[GROUPS : 2 * GROUPS]
                factor_ref[half, block] = jnp.concatenate(
                    [factor, jnp.zeros((8 - GROUPS, 128), F32)], axis=0
                )
        sum_ref[...] = jnp.zeros_like(sum_ref)

    at = lax.broadcasted_iota(jnp.int32, (16, ROWS), 0)
    for half, e_ref in enumerate((e0_ref, e1_ref)):
        mine = factor_ref[half, u]
        row = jnp.concatenate([mine[g : g + 1] for g in range(GROUPS)], axis=1)
        high = row.astype(BF16).astype(F32)
        left = jnp.where(at == 0, high, jnp.where(at == 1, row - high, 0.0)).astype(BF16)
        sum_ref[half] += jnp.dot(left, e_ref[...], preferred_element_type=F32)

    @pl.when(u == QB - 1)
    def _():
        for half in range(2):
            whole = sum_ref[half, 0:1] + sum_ref[half, 1:2]
            for b in range(4):
                row = whole[:, b * ROWS : (b + 1) * ROWS]
                column_ref[0, pl.ds(place_ref[1] ^ KEY_BITS[half][b], 1)] = row
        for to in range(1, KB):
            column_ref[to] = column_ref[0]


def columns(place, expos, stats, all_stats):
    return pl.pallas_call(
        column_kernel,
        grid=(QB,),
        in_specs=[SMEM, EXPO, EXPO, VMEM, VMEM, VMEM],
        out_specs=[VMEM, VMEM],
        out_shape=[
            jax.ShapeDtypeStruct((2, QB, 8, 128), F32),
            jax.ShapeDtypeStruct((KB, KB, ROWS), F32),
        ],
        scratch_shapes=[pltpu.VMEM((2, 16, HALF), F32)],
        compiler_params=pltpu.CompilerParams(vmem_limit_bytes=16 * 1024 * 1024),
    )(place, *expos, *stats, all_stats)


def value_kernel(place_ref, e0_ref, e1_ref, factor_ref, *refs):
    kv_refs, (sums_ref, out_ref, scaled, inverse) = refs[:KB], refs[KB:]
    u = pl.program_id(0)

    @pl.when(u == 0)
    def _():
        inverse[...] = (1.0 / LIFT) / functools.reduce(
            jnp.add, [sums_ref[j] for j in range(KB)]
        )
        bits = KEY_BITS[0] + KEY_BITS[1]
        rows = jnp.concatenate(
            [inverse[pl.ds(place_ref[1] ^ bit, 1)] for bit in bits], axis=0
        )
        for g in range(GROUPS):
            column = rows_to_columns(rows[:, g * 128 : (g + 1) * 128])
            for b in range(KB):
                part = kv_refs[b][1, g * 128 : (g + 1) * 128, :].astype(F32)
                scaled[b * ROWS + g * 128 : b * ROWS + (g + 1) * 128, :] = (
                    part * column[:, b : b + 1]
                ).astype(BF16)

    parts = []
    for half, e_ref in enumerate((e0_ref, e1_ref)):
        part = jnp.dot(
            e_ref[...], scaled[half * HALF : (half + 1) * HALF], preferred_element_type=F32
        )
        parts.append((part, rows_to_columns(factor_ref[half, u]) * LIFT))
    at = place_ref[0] ^ ((u % 2) * 2 + u // 2)
    for g in range(GROUPS):
        rows = slice(g * 128, (g + 1) * 128)
        out_ref[at, rows, :] = sum(
            part[rows] * column[:, g : g + 1] for part, column in parts
        ).astype(BF16)


def attend(place, expos, factor, pieces, sums):
    return pl.pallas_call(
        value_kernel,
        grid=(QB,),
        in_specs=[SMEM, EXPO, EXPO] + [VMEM] * (KB + 2),
        out_specs=VMEM,
        out_shape=jax.ShapeDtypeStruct((QB, ROWS, DIM), BF16),
        scratch_shapes=[pltpu.VMEM((2 * HALF, DIM), BF16), pltpu.VMEM((KB, ROWS), F32)],
        compiler_params=pltpu.CompilerParams(vmem_limit_bytes=16 * 1024 * 1024),
    )(place, *expos, factor, *pieces, sums)


def project_kernel(dzh, place_ref, own_ref, other_ref, w0_ref, w1_ref, out_ref, w_ref):
    zh, core = place_ref[2], place_ref[4]
    for x in range(4):
        head = (zh ^ dzh) * 8 + x * 2 + core
        lanes = pl.ds(pl.multiple_of(head * 128, 128), 128)
        at = slice(x * 128, (x + 1) * 128)
        w_ref[:DIM, at] = w0_ref[:, lanes]
        w_ref[DIM:, at] = w1_ref[:, lanes]
    rows = jnp.concatenate([own_ref[...], other_ref[...]], axis=1)
    part = jnp.dot(rows, w_ref[...], preferred_element_type=F32)
    for x in range(4):
        out_ref[x] = part[:, x * 128 : (x + 1) * 128].astype(BF16)


def project(dzh, place, own, other, w_own, w_other):
    return pl.pallas_call(
        functools.partial(project_kernel, dzh),
        in_specs=[SMEM] + [VMEM] * 4,
        out_specs=VMEM,
        out_shape=jax.ShapeDtypeStruct((4, ROWS, 128), BF16),
        scratch_shapes=[pltpu.VMEM((2 * DIM, 512), BF16)],
        compiler_params=pltpu.CompilerParams(vmem_limit_bytes=16 * 1024 * 1024),
        cost_estimate=pl.CostEstimate(flops=10**10, bytes_accessed=10**6, transcendentals=0),
    )(place, own, other, w_own, w_other)


def query_pair_kernel(a_ref, b_ref, out_ref):
    out_ref[0] = a_ref[0]
    out_ref[1] = b_ref[0]


def query_pair(a, b):
    return pl.pallas_call(
        query_pair_kernel,
        in_specs=[VMEM] * 2,
        out_specs=VMEM,
        out_shape=jax.ShapeDtypeStruct((2, ROWS, DIM), BF16),
        compiler_params=pltpu.CompilerParams(vmem_limit_bytes=8 * 1024 * 1024),
        cost_estimate=pl.CostEstimate(flops=2 * 10**10, bytes_accessed=10**6, transcendentals=0),
    )(a, b)


def shards(query_rows, key_rows, value_rows, out_weight):
    q, k, v = (rows.reshape(1, ROWS, DIM) for rows in (query_rows, key_rows, value_rows))
    ctx, head = lax.axis_index("ctx"), lax.axis_index("head")
    place = jnp.stack(
        [ctx % 4, ctx // 4, head // 8, head // 2 % 4, head % 2]
    ).astype(jnp.int32)
    pair, q = lax.optimization_barrier((jnp.concatenate([k, v]), q))
    far = ctx_send(pair, dza=1)
    q_two = query_pair(q, ctx_send(q, dzb=2))
    near_pieces = [pair] + [ctx_send(pair, dy=bits) for bits in (1, 2, 3)]
    queries = [q_two, ctx_send(q_two, dzb=1)]
    far_pieces = [far] + [ctx_send(far, dy=bits) for bits in (1, 2, 3)]

    expo_near, stats_near = first_scores(queries, near_pieces)
    w_other = head_send(out_weight, dcore=1)
    far_pieces, w_other, stats_near = lax.optimization_barrier((far_pieces, w_other, stats_near))
    expo_far, stats_far, stats = second_scores(place, queries, far_pieces, stats_near)
    expos = (expo_near, expo_far)
    factor, sums = columns(place, expos, (stats_near, stats_far), swap(stats, "ctx", LINE))
    attended = attend(place, expos, factor, near_pieces + far_pieces, swap(sums, "ctx", PLANE))
    whole = jnp.sum(swap(attended, "ctx", LINE).astype(F32), axis=0).astype(BF16)
    other = head_send(whole, dcore=1)
    far = project(1, place, whole, other, out_weight, w_other)
    far = jnp.sum(swap(far, "head", ROW).astype(F32), axis=0).astype(BF16)
    whole, other, far = lax.optimization_barrier((whole, other, far))
    far = head_send(far, dzh=1)
    near = project(0, place, whole, other, out_weight, w_other)
    near = jnp.sum(swap(near, "head", ROW).astype(F32), axis=0)
    return (near + far.astype(F32)).astype(BF16)


def solution(mesh):
    placed = (
        P("ctx", "head", None),
        P("ctx", "head", None),
        P("ctx", "head", None),
        P("head", None),
    )
    return jax.shard_map(
        shards, mesh=mesh, in_specs=placed, out_specs=P("ctx", "head"), check_vma=False
    )
```

```python
import functools
import math

import jax
import jax.numpy as jnp
from jax import lax
from jax.experimental import pallas as pl
from jax.experimental.pallas import tpu as pltpu
from jax.sharding import PartitionSpec as P

F32 = jnp.float32
BF16 = jnp.bfloat16
ROWS = 384
DIM = 128
QB = 4
KB = 8
HALF = 4 * ROWS
KEY_BITS = ((0, 2, 4, 6), (1, 3, 5, 7))
QUERY_BITS = (0, 2, 1, 3)
GROUPS = ROWS // 128
SUB = 128
EXP_SCALE = DIM ** -0.5 * math.log2(math.e)
LIFT = 2.0 ** 20
NT = (((1,), (1,)), ((), ()))
VMEM = pl.BlockSpec(memory_space=pltpu.VMEM)


def ctx_send(value, dy=0, dza=0, dzb=0):
    step = dy * 8 + dza * 4 + dzb
    return lax.ppermute(value, "ctx", [(i, i ^ step) for i in range(32)])


def head_send(value, dzh=0, dx=0, dcore=0):
    step = dzh * 8 + dx * 2 + dcore
    return lax.ppermute(value, "head", [(i, i ^ step) for i in range(16)])


LINE = [[y * 8 + za * 4 + zb for zb in range(4)] for y in range(4) for za in range(2)]
PLANE = [[y * 8 + za * 4 + zb for y in range(4) for za in range(2)] for zb in range(4)]
ROW = [[zh * 8 + x * 2 + core for x in range(4)] for zh in range(2) for core in range(2)]


def swap(value, axis, groups):
    return lax.all_to_all(value, axis, 0, 0, axis_index_groups=groups, tiled=True)


def columns_to_rows(columns):
    lane = lax.broadcasted_iota(jnp.int32, (128, 128), 1)
    square = jnp.zeros((128, 128), F32)
    for at, column in enumerate(columns):
        square = jnp.where(lane == at, column, square)
    return square.T[:8]


def rows_to_columns(rows):
    return jnp.concatenate([rows] * 16, axis=0).T


def gather_queries(u, q_refs, q_all):
    @pl.when(u == 0)
    def _():
        for at in range(QB):
            q_all[at] = q_refs[at // 2][at % 2]


def half_scores(u, q_all, kv_refs, e_ref, s_ref):
    peaks, totals = [], []
    for sub in range(GROUPS):
        q = q_all[u, sub * SUB : (sub + 1) * SUB, :]
        top = jnp.full((SUB, 128), -jnp.inf, F32)
        for b in range(4):
            s = lax.dot_general(q, kv_refs[b][0], NT, preferred_element_type=F32)
            s_ref[sub, :, b * ROWS : (b + 1) * ROWS] = s
            for g in range(GROUPS):
                top = jnp.maximum(top, s[:, g * 128 : (g + 1) * 128])
        peak = jnp.max(top, axis=1, keepdims=True)
        total = jnp.zeros((SUB, 128), F32)
        for b in range(4 * GROUPS):
            e = jnp.exp2((s_ref[sub, :, b * 128 : (b + 1) * 128] - peak) * EXP_SCALE)
            total = total + e
            e_ref[sub * SUB : (sub + 1) * SUB, b * 128 : (b + 1) * 128] = e.astype(BF16)
        peaks.append(peak)
        totals.append(jnp.sum(total, axis=1, keepdims=True))
    return columns_to_rows(peaks + totals)


def first_score_kernel(*refs):
    q_refs, kv_refs, (e_ref, stat_ref, q_all, s_ref) = refs[:2], refs[2:6], refs[6:]
    u = pl.program_id(0)
    gather_queries(u, q_refs, q_all)
    stat_ref[u] = half_scores(u, q_all, kv_refs, e_ref, s_ref)


def combine(a, b):
    peak = jnp.maximum(a[:GROUPS], b[:GROUPS])
    total = a[GROUPS : 2 * GROUPS] * jnp.exp2((a[:GROUPS] - peak) * EXP_SCALE)
    total = total + b[GROUPS : 2 * GROUPS] * jnp.exp2((b[:GROUPS] - peak) * EXP_SCALE)
    return jnp.concatenate([peak, total, jnp.zeros((8 - 2 * GROUPS, 128), F32)], axis=0)


def second_score_kernel(place_ref, *refs):
    q_refs, kv_refs, first_ref = refs[:2], refs[2:6], refs[6]
    e_ref, stat_ref, both_ref, q_all, s_ref = refs[7:]
    u = pl.program_id(0)
    gather_queries(u, q_refs, q_all)
    rows = half_scores(u, q_all, kv_refs, e_ref, s_ref)
    stat_ref[u] = rows
    rows = combine(first_ref[u], rows)
    at = place_ref[0] ^ ((u % 2) * 2 + u // 2)
    for to in range(QB):
        both_ref[to, at] = rows


SMEM = pl.BlockSpec(memory_space=pltpu.SMEM)
EXPO = pl.BlockSpec((ROWS, HALF), lambda u: (u, 0))
SCORE = dict(
    grid=(QB,),
    scratch_shapes=[pltpu.VMEM((QB, ROWS, DIM), BF16), pltpu.VMEM((GROUPS, SUB, HALF), F32)],
    compiler_params=pltpu.CompilerParams(vmem_limit_bytes=16 * 1024 * 1024),
)
EXPO_TYPE = jax.ShapeDtypeStruct((QB * ROWS, HALF), BF16)
STAT_TYPE = jax.ShapeDtypeStruct((QB, 8, 128), F32)


def first_scores(queries, pieces):
    return pl.pallas_call(
        first_score_kernel,
        in_specs=[VMEM] * 6,
        out_specs=[EXPO, VMEM],
        out_shape=[EXPO_TYPE, STAT_TYPE],
        **SCORE,
    )(*queries, *pieces)


def second_scores(place, queries, pieces, stats):
    return pl.pallas_call(
        second_score_kernel,
        in_specs=[SMEM] + [VMEM] * 7,
        out_specs=[EXPO, VMEM, VMEM],
        out_shape=[EXPO_TYPE, STAT_TYPE, jax.ShapeDtypeStruct((QB, QB, 8, 128), F32)],
        **SCORE,
    )(place, *queries, *pieces, stats)


def column_kernel(
    place_ref, e0_ref, e1_ref, stat0_ref, stat1_ref, all_ref, factor_ref, column_ref, sum_ref
):
    u = pl.program_id(0)

    @pl.when(u == 0)
    def _():
        for block in range(QB):
            at = place_ref[0] ^ QUERY_BITS[block]
            whole = functools.reduce(combine, [all_ref[j, at] for j in range(QB)])
            for half, stat_ref in enumerate((stat0_ref, stat1_ref)):
                mine = stat_ref[block]
                factor = jnp.exp2((mine[:GROUPS] - whole[:GROUPS]) * EXP_SCALE)
                factor = factor / whole[GROUPS : 2 * GROUPS]
                factor_ref[half, block] = jnp.concatenate(
                    [factor, jnp.zeros((8 - GROUPS, 128), F32)], axis=0
                )
        sum_ref[...] = jnp.zeros_like(sum_ref)

    at = lax.broadcasted_iota(jnp.int32, (16, ROWS), 0)
    for half, e_ref in enumerate((e0_ref, e1_ref)):
        mine = factor_ref[half, u]
        row = jnp.concatenate([mine[g : g + 1] for g in range(GROUPS)], axis=1)
        high = row.astype(BF16).astype(F32)
        left = jnp.where(at == 0, high, jnp.where(at == 1, row - high, 0.0)).astype(BF16)
        sum_ref[half] += jnp.dot(left, e_ref[...], preferred_element_type=F32)

    @pl.when(u == QB - 1)
    def _():
        for half in range(2):
            whole = sum_ref[half, 0:1] + sum_ref[half, 1:2]
            for b in range(4):
                row = whole[:, b * ROWS : (b + 1) * ROWS]
                column_ref[0, pl.ds(place_ref[1] ^ KEY_BITS[half][b], 1)] = row
        for to in range(1, KB):
            column_ref[to] = column_ref[0]


def columns(place, expos, stats, all_stats):
    return pl.pallas_call(
        column_kernel,
        grid=(QB,),
        in_specs=[SMEM, EXPO, EXPO, VMEM, VMEM, VMEM],
        out_specs=[VMEM, VMEM],
        out_shape=[
            jax.ShapeDtypeStruct((2, QB, 8, 128), F32),
            jax.ShapeDtypeStruct((KB, KB, ROWS), F32),
        ],
        scratch_shapes=[pltpu.VMEM((2, 16, HALF), F32)],
        compiler_params=pltpu.CompilerParams(vmem_limit_bytes=16 * 1024 * 1024),
    )(place, *expos, *stats, all_stats)


def value_kernel(place_ref, e0_ref, e1_ref, factor_ref, *refs):
    kv_refs, (sums_ref, out_ref, scaled, inverse) = refs[:KB], refs[KB:]
    u = pl.program_id(0)

    @pl.when(u == 0)
    def _():
        inverse[...] = (1.0 / LIFT) / functools.reduce(
            jnp.add, [sums_ref[j] for j in range(KB)]
        )
        bits = KEY_BITS[0] + KEY_BITS[1]
        rows = jnp.concatenate(
            [inverse[pl.ds(place_ref[1] ^ bit, 1)] for bit in bits], axis=0
        )
        for g in range(GROUPS):
            column = rows_to_columns(rows[:, g * 128 : (g + 1) * 128])
            for b in range(KB):
                part = kv_refs[b][1, g * 128 : (g + 1) * 128, :].astype(F32)
                scaled[b * ROWS + g * 128 : b * ROWS + (g + 1) * 128, :] = (
                    part * column[:, b : b + 1]
                ).astype(BF16)

    parts = []
    for half, e_ref in enumerate((e0_ref, e1_ref)):
        part = jnp.dot(
            e_ref[...], scaled[half * HALF : (half + 1) * HALF], preferred_element_type=F32
        )
        parts.append((part, rows_to_columns(factor_ref[half, u]) * LIFT))
    at = place_ref[0] ^ ((u % 2) * 2 + u // 2)
    for g in range(GROUPS):
        rows = slice(g * 128, (g + 1) * 128)
        out_ref[at, rows, :] = sum(
            part[rows] * column[:, g : g + 1] for part, column in parts
        ).astype(BF16)


def attend(place, expos, factor, pieces, sums):
    return pl.pallas_call(
        value_kernel,
        grid=(QB,),
        in_specs=[SMEM, EXPO, EXPO] + [VMEM] * (KB + 2),
        out_specs=VMEM,
        out_shape=jax.ShapeDtypeStruct((QB, ROWS, DIM), BF16),
        scratch_shapes=[pltpu.VMEM((2 * HALF, DIM), BF16), pltpu.VMEM((KB, ROWS), F32)],
        compiler_params=pltpu.CompilerParams(vmem_limit_bytes=16 * 1024 * 1024),
    )(place, *expos, factor, *pieces, sums)


def project_kernel(dzh, place_ref, own_ref, other_ref, w0_ref, w1_ref, out_ref, w_ref):
    zh, core = place_ref[2], place_ref[4]
    for x in range(4):
        head = (zh ^ dzh) * 8 + x * 2 + core
        lanes = pl.ds(pl.multiple_of(head * 128, 128), 128)
        at = slice(x * 128, (x + 1) * 128)
        w_ref[:DIM, at] = w0_ref[:, lanes]
        w_ref[DIM:, at] = w1_ref[:, lanes]
    rows = jnp.concatenate([own_ref[...], other_ref[...]], axis=1)
    part = jnp.dot(rows, w_ref[...], preferred_element_type=F32)
    for x in range(4):
        out_ref[x] = part[:, x * 128 : (x + 1) * 128].astype(BF16)


def project(dzh, place, own, other, w_own, w_other):
    return pl.pallas_call(
        functools.partial(project_kernel, dzh),
        in_specs=[SMEM] + [VMEM] * 4,
        out_specs=VMEM,
        out_shape=jax.ShapeDtypeStruct((4, ROWS, 128), BF16),
        scratch_shapes=[pltpu.VMEM((2 * DIM, 512), BF16)],
        compiler_params=pltpu.CompilerParams(vmem_limit_bytes=16 * 1024 * 1024),
        cost_estimate=pl.CostEstimate(flops=10**10, bytes_accessed=10**6, transcendentals=0),
    )(place, own, other, w_own, w_other)


def query_pair_kernel(a_ref, b_ref, out_ref):
    out_ref[0] = a_ref[0]
    out_ref[1] = b_ref[0]


def query_pair(a, b):
    return pl.pallas_call(
        query_pair_kernel,
        in_specs=[VMEM] * 2,
        out_specs=VMEM,
        out_shape=jax.ShapeDtypeStruct((2, ROWS, DIM), BF16),
        compiler_params=pltpu.CompilerParams(vmem_limit_bytes=8 * 1024 * 1024),
        cost_estimate=pl.CostEstimate(flops=2 * 10**10, bytes_accessed=10**6, transcendentals=0),
    )(a, b)


def shards(query_rows, key_rows, value_rows, out_weight):
    q, k, v = (rows.reshape(1, ROWS, DIM) for rows in (query_rows, key_rows, value_rows))
    ctx, head = lax.axis_index("ctx"), lax.axis_index("head")
    place = jnp.stack(
        [ctx % 4, ctx // 4, head // 8, head // 2 % 4, head % 2]
    ).astype(jnp.int32)
    pair, q = lax.optimization_barrier((jnp.concatenate([k, v]), q))
    far = ctx_send(pair, dza=1)
    q_two = query_pair(q, ctx_send(q, dzb=2))
    near_pieces = [pair] + [ctx_send(pair, dy=bits) for bits in (1, 2, 3)]
    queries = [q_two, ctx_send(q_two, dzb=1)]
    far_pieces = [far] + [ctx_send(far, dy=bits) for bits in (1, 2, 3)]

    expo_near, stats_near = first_scores(queries, near_pieces)
    w_other = head_send(out_weight, dcore=1)
    far_pieces, w_other, stats_near = lax.optimization_barrier((far_pieces, w_other, stats_near))
    expo_far, stats_far, stats = second_scores(place, queries, far_pieces, stats_near)
    expos = (expo_near, expo_far)
    factor, sums = columns(place, expos, (stats_near, stats_far), swap(stats, "ctx", LINE))
    attended = attend(place, expos, factor, near_pieces + far_pieces, swap(sums, "ctx", PLANE))
    whole = jnp.sum(swap(attended, "ctx", LINE).astype(F32), axis=0).astype(BF16)
    other = head_send(whole, dcore=1)
    far = project(1, place, whole, other, out_weight, w_other)
    far = jnp.sum(swap(far, "head", ROW).astype(F32), axis=0).astype(BF16)
    whole, other, far = lax.optimization_barrier((whole, other, far))
    far = lax.optimization_barrier(head_send(far, dzh=1).astype(F32))
    near = project(0, place, whole, other, out_weight, w_other)
    near = jnp.sum(swap(near, "head", ROW).astype(F32), axis=0)
    return (near + far).astype(BF16)


def solution(mesh):
    placed = (
        P("ctx", "head", None),
        P("ctx", "head", None),
        P("ctx", "head", None),
        P("head", None),
    )
    return jax.shard_map(
        shards, mesh=mesh, in_specs=placed, out_specs=P("ctx", "head"), check_vma=False
    )
```
